32 devices in a mesh: grp: 2 (over y), sp: 4 (over z), flt: 2 (over x), rep: 2 (over core).
Axes of the slice: x: 2, y: 2, z: 4, core: 2. Of those that a mesh axis runs over, the one named last changes fastest.
Arguments:
- acts: float32 [64, 8, 8, 512], P(None, ('grp', 'sp'), ('flt', 'rep')), parts along dimension 1, may hold values from -6 to 6
- grad_out: float32 [64, 8, 8, 512], P(None, ('grp', 'sp'), ('flt', 'rep')), parts along dimension 1, may hold values from -6 to 6
- kernel: float32 [3, 3, 3, 64, 64], replicated, may hold values from -0.15625 to 0.15625
Outputs:
- input_grad: float32 [64, 8, 8, 512], P(None, ('grp', 'sp'), ('flt', 'rep')), parts along dimension 1
- weight_grad: float32 [6, 3, 3, 64, 64], P('grp'), parts along dimension 0
The draws below stay inside these ranges and needn't reach their ends.
There are 2 independent parts, one for each index of `grp`. The reference program is written for one: setup_inputs(seed, part) draws one part's arguments, and reference() takes and returns one part's arrays. A program takes and returns all parts, laid end to end along the dimension named above; an argument that names none is the same for every part. Nothing has to cross between parts.
All inputs are finite; a program needn't handle non-finite values.
Results may differ from the reference program's by a relative error of at most 0.00007.
Values sent between devices are 32-bit elements; how exact they have to be, the bound alone decides.
A program may use at most 64 MiB of HBM per device.

```python
import math
import jax
import jax.numpy as jnp
from jax import lax

CIN = 64
COUT = 64
XN = 512
ZN = 4
YN = 8
VOXELS = 16384


def shard_levels(key, extent, split, least, top_value):
    gain, own = 1.0, jax.random.fold_in(key, 6)
    for position, shards_of in split:
        draws = jnp.exp(jax.random.uniform(jax.random.fold_in(own, position), (shards_of,), jnp.float32, least / len(split), top_value / len(split)))
        gain = gain * jnp.repeat(draws, extent[position] // shards_of).reshape([-1 if axis == position else 1 for axis in range(len(extent))])
    return gain


def normal_values(key, extent, spread, most, split=(), held_as=jnp.bfloat16):
    values = spread * jax.random.normal(key, extent, jnp.float32)
    if split:
        values = values * shard_levels(key, extent, split, -0.22, 0.18)
    return jnp.clip(values, -most, most).astype(held_as)


def setup_inputs(seed: int = 0, part: int = 0) -> dict:
    splits = jax.random.split(jax.random.key(seed), 4)
    part_splits = jax.random.split(jax.random.fold_in(splits[3], part), 4)
    return {
        "acts": normal_values(part_splits[0], (CIN, ZN, YN, XN), 1.0, 6.0, ((1, 4), (2, 4)), jnp.float32),
        "grad_out": normal_values(part_splits[1], (COUT, ZN, YN, XN), 1.0, 6.0, ((1, 4), (2, 4)), jnp.float32),
        "kernel": normal_values(splits[2], (3, 3, 3, CIN, COUT), (27 * CIN) ** -0.5, 0.15625, (), jnp.float32),
    }


def forward(acts, kernel):
    out = lax.conv_general_dilated(acts[None], kernel, (1, 1, 1), 'SAME', dimension_numbers=('NCDHW', 'DHWIO', 'NCDHW'), precision=lax.Precision.HIGHEST)
    return out[0]

def reference(acts, grad_out, kernel):
    result, pullback = jax.vjp(forward, acts, kernel)
    input_grad, weight_grad = pullback(grad_out)
    factor = 1.0 / math.sqrt(VOXELS)
    return (input_grad, weight_grad * factor)
```

```python
import functools
import math

import jax
import jax.numpy as jnp
from jax import lax
from jax.experimental import pallas as pl
from jax.experimental.pallas import tpu as pltpu
from jax.sharding import PartitionSpec as P

MESH = pl.DeviceIdType.MESH
VMEM = pltpu.VMEM


class Group:
    def __init__(self, sp, flt):
        self.flt, self.count = flt, sp * flt
        self.core = lax.axis_index("rep")
        self.chip = lax.axis_index("sp") * flt + lax.axis_index("flt")

    def peer(self, chip):
        return {"sp": chip // self.flt, "flt": chip % self.flt}

    def partner(self):
        return {"rep": 1 - self.core}

    def after(self, step):
        return lax.rem(self.chip + 1 + step, self.count)

    def before(self, step):
        return lax.rem(self.chip + 2 * self.count - 1 - step, self.count)


def sum_over_group(group, piece, terms, held, arrived, total, sems):
    core, chip, count = group.core, group.chip, group.count
    half = count * piece

    def rows(at):
        return pl.ds(pl.multiple_of(at, 8), piece)

    def to_partner(j):
        return pltpu.make_async_remote_copy(
            terms.at[rows((1 - core) * half + j * piece)],
            held.at[rows(j * piece)],
            sems.at[0, j],
            sems.at[1, j],
            device_id=group.partner(),
            device_id_type=MESH,
        )

    def scatter(j, slot):
        return pltpu.make_async_remote_copy(
            held.at[rows(j * piece)],
            arrived.at[rows(slot * piece)],
            sems.at[2, j],
            sems.at[3, slot],
            device_id=group.peer(j),
            device_id_type=MESH,
        )

    def gather(j, slot):
        part = total.at[rows(core * half + slot * piece)]
        return pltpu.make_async_remote_copy(
            part,
            part,
            sems.at[4, j],
            sems.at[5, slot],
            device_id=group.peer(j),
            device_id_type=MESH,
        )

    def pass_on(j, owner):
        part = total.at[rows(owner * half + j * piece)]
        return pltpu.make_async_remote_copy(
            part,
            part,
            sems.at[6, j],
            sems.at[7, j],
            device_id=group.partner(),
            device_id_type=MESH,
        )

    def each(steps, body):
        def run(step, carry):
            body(step)
            return carry

        lax.fori_loop(0, steps, run, 0)

    def start():
        each(count, lambda k: to_partner(group.after(k)).start())

    def add_and_scatter(k):
        j = group.after(k)
        to_partner(j).wait_recv()
        own = rows(j * piece)
        held[own, :] = held[own, :] + terms[rows(core * half + j * piece), :]

        @pl.when(k < count - 1)
        def _():
            scatter(j, chip).start()

    def add_arrived(k):
        j = group.before(k)
        scatter(j, j).wait_recv()
        own = rows(chip * piece)
        held[own, :] = held[own, :] + arrived[rows(j * piece), :]

    def middle():
        each(count, add_and_scatter)

    def forward(k):
        j = group.before(k)
        gather(j, j).wait_recv()
        pass_on(j, core).start()

    def finish():
        each(count - 1, add_arrived)
        total[rows(core * half + chip * piece), :] = held[rows(chip * piece), :]
        each(count - 1, lambda k: gather(group.after(k), chip).start())
        pass_on(chip, core).start()
        each(count - 1, forward)
        each(count, lambda k: pass_on(k, 1 - core).wait_recv())
        each(count, lambda k: to_partner(k).wait_send())
        each(count, lambda k: pass_on(k, core).wait_send())

        def sent(k):
            j = group.after(k)
            scatter(j, chip).wait_send()
            gather(j, chip).wait_send()

        each(count - 1, sent)

    return start, middle, finish


def greet(devices):
    barrier = pltpu.get_barrier_semaphore()
    for device in devices:
        pl.semaphore_signal(barrier, 1, device_id=device, device_id_type=MESH)
    return barrier


def greet_group(group):
    barrier = greet([group.partner()])

    def run(k, carry):
        pl.semaphore_signal(
            barrier, 1, device_id=group.peer(group.after(k)), device_id_type=MESH
        )
        return carry

    lax.fori_loop(0, group.count - 1, run, 0)
    pl.semaphore_wait(barrier, group.count)


def reduce_kernel(sp, flt, piece, terms, total, held, arrived, sems):
    group = Group(sp, flt)
    greet_group(group)
    start, middle, finish = sum_over_group(group, piece, terms, held, arrived, total, sems)
    start()
    middle()
    finish()


def reduced(term, cin, cout):
    sp, flt = lax.axis_size("sp"), lax.axis_size("flt")
    count = sp * flt
    size = term.size // 256
    piece = -(-size // (8 * count)) * 8
    half = count * piece
    packed = term.reshape(2, size, 128)
    packed = jnp.pad(packed, ((0, 0), (0, half - size), (0, 0))).reshape(2 * half, 128)
    out = pl.pallas_call(
        functools.partial(reduce_kernel, sp, flt, piece),
        out_shape=jax.ShapeDtypeStruct(packed.shape, jnp.float32),
        in_specs=[pl.BlockSpec(memory_space=VMEM)],
        out_specs=pl.BlockSpec(memory_space=VMEM),
        scratch_shapes=[
            VMEM((half, 128), jnp.float32),
            VMEM((half, 128), jnp.float32),
            pltpu.SemaphoreType.DMA((8, count)),
        ],
        compiler_params=pltpu.CompilerParams(collective_id=0, has_side_effects=True, vmem_limit_bytes=32 * 2**20),
    )(packed)
    return out.reshape(2, half, 128)[:, :size].reshape(term.shape)


def padded_2(value, sides, width):
    for axis, dim in sides:
        count, length = (lax.axis_size(axis), value.shape[dim])
        up = [(i, (i + 1) % count) for i in range(count - 1)]
        down = [(j, i) for i, j in up]
        last = lax.slice_in_dim(value, length - width, length, axis=dim)
        first = lax.slice_in_dim(value, 0, width, axis=dim)
        before = lax.ppermute(last, axis, up)
        after = lax.ppermute(first, axis, down)
        value = jnp.concatenate([before, value, after], axis=dim)
    return value


def take_next(values):
    edge = jnp.zeros(values.shape[:-1] + (1,), values.dtype)
    return jnp.concatenate([values[..., 1:], edge], axis=-1)


def take_prior(values):
    edge = jnp.zeros(values.shape[:-1] + (1,), values.dtype)
    return jnp.concatenate([edge, values[..., :-1]], axis=-1)


def contract_last(left, right):
    return lax.dot_general(left, right, (((1,), (1,)), ((), ())), precision=lax.Precision.HIGH)


def per_device(acts, grad_out, kernel):
    cin = acts.shape[0]
    planes = acts.shape[1]
    rows = acts.shape[2]
    width = acts.shape[3]
    cout = grad_out.shape[0]
    voxels = (
        planes * lax.axis_size("sp") * rows * lax.axis_size("flt") * lax.axis_size("rep") * width
    )
    factor = 1.0 / math.sqrt(voxels)
    padded = padded_2(grad_out, (("sp", 1), (("flt", "rep"), 2)), 1)
    weights_tap = kernel.reshape(9, 3 * cin, cout)
    weight_terms = [jnp.zeros((3 * cin, cout), jnp.float32) for index in range(9)]
    source = acts[:, 0]
    source_stack = jnp.concatenate([take_prior(source), source, take_next(source)], axis=0).reshape(
        3 * cin, rows * width
    )
    partial_sum = jnp.zeros((3 * cin, rows * width), jnp.float32)
    for a_tap in range(3):
        for b_tap in range(3):
            index = 3 * a_tap + b_tap
            slab = padded[:, 2 - a_tap, 2 - b_tap : 2 - b_tap + rows, :].reshape(cout, rows * width)
            partial_sum = partial_sum + jnp.dot(
                weights_tap[index], slab, precision=lax.Precision.HIGH
            )
            weight_terms[index] = contract_last(source_stack, slab)
    parts_x = partial_sum.reshape(3, cin, rows, width)
    plane_out = take_next(parts_x[0]) + parts_x[1] + take_prior(parts_x[2])
    outputs = [plane_out]
    term = jnp.stack(weight_terms, axis=0).reshape(3, 3, 3, cin, cout) * factor
    weight_grad = reduced(term, cin, cout)
    input_grad = jnp.stack(outputs, axis=1)
    return (input_grad, weight_grad)


def solution(mesh):
    placed = (
        P(None, ("grp", "sp"), ("flt", "rep"), None),
        P(None, ("grp", "sp"), ("flt", "rep"), None),
        P(),
    )
    return jax.shard_map(
        per_device,
        mesh=mesh,
        in_specs=placed,
        out_specs=(P(None, ("grp", "sp"), ("flt", "rep"), None), P("grp", None, None, None, None)),
        check_vma=False,
    )
```

```python
import functools
import math

import jax
import jax.numpy as jnp
from jax import lax
from jax.experimental import pallas as pl
from jax.experimental.pallas import tpu as pltpu
from jax.sharding import PartitionSpec as P

MESH = pl.DeviceIdType.MESH
VMEM = pltpu.VMEM


class Group:
    def __init__(self, sp, flt):
        self.flt, self.count = flt, sp * flt
        self.core = lax.axis_index("rep")
        self.chip = lax.axis_index("sp") * flt + lax.axis_index("flt")

    def peer(self, chip):
        return {"sp": chip // self.flt, "flt": chip % self.flt}

    def partner(self):
        return {"rep": 1 - self.core}

    def after(self, step):
        return lax.rem(self.chip + 1 + step, self.count)

    def before(self, step):
        return lax.rem(self.chip + 2 * self.count - 1 - step, self.count)


def sum_over_group(group, piece, terms, held, arrived, total, sems):
    core, chip, count = group.core, group.chip, group.count
    half = count * piece

    def rows(at):
        return pl.ds(pl.multiple_of(at, 8), piece)

    def to_partner(j):
        return pltpu.make_async_remote_copy(
            terms.at[rows((1 - core) * half + j * piece)],
            held.at[rows(j * piece)],
            sems.at[0, j],
            sems.at[1, j],
            device_id=group.partner(),
            device_id_type=MESH,
        )

    def scatter(j, slot):
        return pltpu.make_async_remote_copy(
            held.at[rows(j * piece)],
            arrived.at[rows(slot * piece)],
            sems.at[2, j],
            sems.at[3, slot],
            device_id=group.peer(j),
            device_id_type=MESH,
        )

    def gather(j, slot):
        part = total.at[rows(core * half + slot * piece)]
        return pltpu.make_async_remote_copy(
            part,
            part,
            sems.at[4, j],
            sems.at[5, slot],
            device_id=group.peer(j),
            device_id_type=MESH,
        )

    def pass_on(j, owner):
        part = total.at[rows(owner * half + j * piece)]
        return pltpu.make_async_remote_copy(
            part,
            part,
            sems.at[6, j],
            sems.at[7, j],
            device_id=group.partner(),
            device_id_type=MESH,
        )

    def each(steps, body):
        def run(step, carry):
            body(step)
            return carry

        lax.fori_loop(0, steps, run, 0)

    def start():
        each(count, lambda k: to_partner(group.after(k)).start())

    def add_and_scatter(k):
        j = group.after(k)
        to_partner(j).wait_recv()
        own = rows(j * piece)
        held[own, :] = held[own, :] + terms[rows(core * half + j * piece), :]

        @pl.when(k < count - 1)
        def _():
            scatter(j, chip).start()

    def add_arrived(k):
        j = group.before(k)
        scatter(j, j).wait_recv()
        own = rows(chip * piece)
        held[own, :] = held[own, :] + arrived[rows(j * piece), :]

    def middle():
        each(count, add_and_scatter)

    def forward(k):
        j = group.before(k)
        gather(j, j).wait_recv()
        pass_on(j, core).start()

    def finish():
        each(count - 1, add_arrived)
        total[rows(core * half + chip * piece), :] = held[rows(chip * piece), :]
        each(count - 1, lambda k: gather(group.after(k), chip).start())
        pass_on(chip, core).start()
        each(count - 1, forward)
        each(count, lambda k: pass_on(k, 1 - core).wait_recv())
        each(count, lambda k: to_partner(k).wait_send())
        each(count, lambda k: pass_on(k, core).wait_send())

        def sent(k):
            j = group.after(k)
            scatter(j, chip).wait_send()
            gather(j, chip).wait_send()

        each(count - 1, sent)

    return start, middle, finish


def halves(value):
    high = value.astype(jnp.bfloat16)
    return high, (value - high.astype(jnp.float32)).astype(jnp.bfloat16)


def moved(value, step):
    width = value.shape[-1]
    lane = lax.broadcasted_iota(jnp.int32, value.shape, 1)
    edge = 0 if step == 1 else width - 1
    return jnp.where(lane == edge, 0.0, pltpu.roll(value, step % width, 1))


def product(left, right, dims):
    (lh, ll), (rh, rl) = left, right

    def dot(x, y):
        return lax.dot_general(x, y, (dims, ((), ())), preferred_element_type=jnp.float32)

    return dot(lh, rh) + dot(lh, rl) + dot(ll, rh)


def backward_kernel(
    sp, flt, piece, size, factor, acts, grad, weights, out, wgrad,
    pad, high, low, acts_high, acts_low, w_high, w_low,
    terms, held, arrived, total, send, recv, sems,
):
    group = Group(sp, flt)
    core, count = group.core, group.count
    z, x = lax.axis_index("sp"), lax.axis_index("flt")
    cin, width = acts.shape[1:]
    cout = grad.shape[1]
    half = count * piece
    z_exists = {0: z > 0, 2: z < sp - 1}
    cross_x = x + 2 * core - 1
    cross_exists = (cross_x >= 0) & (cross_x < flt)
    cross = {"flt": cross_x, "rep": 1 - core}

    barrier = pltpu.get_barrier_semaphore()
    pl.semaphore_signal(barrier, 1, device_id=group.partner(), device_id_type=MESH)

    def signal(k, carry):
        pl.semaphore_signal(
            barrier, 1, device_id=group.peer(group.after(k)), device_id_type=MESH
        )
        return carry

    lax.fori_loop(0, count - 1, signal, 0)

    @pl.when(cross_exists)
    def _():
        pl.semaphore_signal(barrier, 1, device_id=cross, device_id_type=MESH)
        pl.semaphore_wait(barrier, count + 1)

    @pl.when(jnp.logical_not(cross_exists))
    def _():
        pl.semaphore_wait(barrier, count)

    def copy(src, index, slot, device):
        return pltpu.make_async_remote_copy(
            src, pad.at[index], send.at[slot], recv.at[index],
            device_id=device, device_id_type=MESH,
        )

    def to_z(plane, row):
        return copy(grad.at[row], (2 - plane) * 4 + 1 + row, plane + row, {"sp": z + plane - 1})

    def edge(plane, row):
        return grad.at[row - 1] if plane == 1 else pad.at[plane * 4 + row]

    def to_cross(plane):
        return copy(edge(plane, 1 + core), plane * 4 + 3 * (1 - core), 4 + plane, cross)

    def to_partner(plane):
        return copy(edge(plane, 2 - core), plane * 4 + 3 * core, 7 + plane, group.partner())

    def await_row(plane, row):
        index = plane * 4 + row
        copy(grad.at[0], index, 0, group.partner()).wait_recv()

    for plane in (0, 2):

        @pl.when(z_exists[plane])
        def _():
            to_z(plane, core).start()

    @pl.when(cross_exists)
    def _():
        to_cross(1).start()

    to_partner(1).start()
    for plane in (0, 2):

        @pl.when(z_exists[plane])
        def _():
            to_z(plane, 1 - core).start()

    def keep(plane, row, value):
        at = pl.ds(pl.multiple_of(row * cout, cout), cout)
        high[plane, at, :], low[plane, at, :] = halves(value)

    for row in range(2):
        keep(1, 1 + row, grad[row])
        line = acts[row]
        for c, value in enumerate((moved(line, 1), line, moved(line, -1))):
            at = pl.ds(c * cin, cin)
            acts_high[row, at, :], acts_low[row, at, :] = halves(value)
    for a in range(3):
        for c in range(3):
            taps = jnp.concatenate([weights[9 * a + 3 * b + c] for b in (2, 1, 0)], axis=1)
            at = pl.ds(c * cin, cin)
            w_high[a, at, :], w_low[a, at, :] = halves(taps)

    def place(row):
        return row if row < size else row - size + half

    def put(row, value):
        rows = value.shape[0]
        first = min(max(size - row, 0), rows)
        if first:
            terms[pl.ds(row, first), :] = value[:first]
        if rows - first:
            terms[pl.ds(place(row + first), rows - first), :] = value[first:]

    if half > size:
        for owner in range(2):
            terms[pl.ds(owner * half + size, half - size), :] = jnp.zeros(
                (half - size, 128), jnp.float32
            )

    blocks = 3 * cout
    each_tap = 9 * cin * cout // 128

    def weight_terms(a):
        plane = 2 - a
        result = jnp.zeros((3 * cin, blocks), jnp.float32)
        for row in range(2):
            at = pl.ds(row * cout, blocks)
            result = result + product(
                (acts_high[row], acts_low[row]),
                (high[plane, at, :], low[plane, at, :]),
                ((1,), (1,)),
            )
        put(a * each_tap, result[:, :128])
        rest = result[:, 128:]
        middle = 3 * cin // 2
        put(a * each_tap + 3 * cin, jnp.concatenate([rest[:middle], rest[middle:]], axis=1))

    def take(plane, row, exists):
        @pl.when(exists)
        def _():
            await_row(plane, row)
            keep(plane, row, pad[plane * 4 + row])

        @pl.when(jnp.logical_not(exists))
        def _():
            keep(plane, row, jnp.zeros((cout, width), jnp.float32))

    always = z >= 0
    for plane in (0, 2):

        @pl.when(z_exists[plane])
        def _():
            await_row(plane, 1 + core)

            @pl.when(cross_exists)
            def _():
                to_cross(plane).start()

    take(1, 3 * (1 - core), always)
    take(1, 3 * core, cross_exists)
    weight_terms(1)
    for plane in (0, 2):

        @pl.when(z_exists[plane])
        def _():
            await_row(plane, 2 - core)
            to_partner(plane).start()
            keep(plane, 1, pad[plane * 4 + 1])
            keep(plane, 2, pad[plane * 4 + 2])

        @pl.when(jnp.logical_not(z_exists[plane]))
        def _():
            for row in (1, 2):
                keep(plane, row, jnp.zeros((cout, width), jnp.float32))

    for plane in (0, 2):
        take(plane, 3 * (1 - core), z_exists[plane])
        take(plane, 3 * core, z_exists[plane] & cross_exists)
        weight_terms(2 - plane)

    start, middle, finish = sum_over_group(group, piece, terms, held, arrived, total, sems)
    start()
    middle()
    for row in range(2):
        at = pl.ds(row * cout, blocks)
        result = jnp.zeros((3 * cin, width), jnp.float32)
        for a in range(3):
            result = result + product(
                (w_high[a], w_low[a]), (high[2 - a, at, :], low[2 - a, at, :]), ((1,), (0,))
            )
        out[row] = (
            moved(result[:cin], -1) + result[cin : 2 * cin] + moved(result[2 * cin :], 1)
        )
    for plane in (0, 2):

        @pl.when(z_exists[plane])
        def _():
            to_z(plane, core).wait_send()
            to_z(plane, 1 - core).wait_send()
            to_partner(plane).wait_send()

        @pl.when(z_exists[plane] & cross_exists)
        def _():
            to_cross(plane).wait_send()

    to_partner(1).wait_send()

    @pl.when(cross_exists)
    def _():
        to_cross(1).wait_send()

    finish()
    step = 16
    for a in range(3):
        for c in range(3):
            for i in range(0, cin, step):
                line = c * cin + i
                both = total[pl.ds(place(a * each_tap + line), step), :] * factor
                wrapped, lane = line % (3 * cin // 2), line // (3 * cin // 2) * cout
                last = total[pl.ds(place(a * each_tap + 3 * cin + wrapped), step), :] * factor
                at = pl.ds(i, step)
                wgrad[9 * a + 6 + c, at, :] = both[:, :cout]
                wgrad[9 * a + 3 + c, at, :] = both[:, cout:]
                wgrad[9 * a + c, at, :] = last[:, lane : lane + cout]


def per_device(acts, grad_out, kernel):
    cin, planes, rows, width = acts.shape
    cout = grad_out.shape[0]
    sp, flt = lax.axis_size("sp"), lax.axis_size("flt")
    count = sp * flt
    voxels = planes * sp * rows * flt * lax.axis_size("rep") * width
    factor = 1.0 / math.sqrt(voxels)
    size = kernel.size // 256
    piece = -(-size // (8 * count)) * 8
    half = count * piece
    f32, bf16 = jnp.float32, jnp.bfloat16
    vmem = pl.BlockSpec(memory_space=VMEM)
    out, wgrad = pl.pallas_call(
        functools.partial(backward_kernel, sp, flt, piece, size, factor),
        out_shape=(
            jax.ShapeDtypeStruct((rows, cin, width), f32),
            jax.ShapeDtypeStruct((27, cin, cout), f32),
        ),
        in_specs=[vmem] * 3,
        out_specs=(vmem, vmem),
        scratch_shapes=[
            VMEM((12, cout, width), f32),
            VMEM((3, 4 * cout, width), bf16),
            VMEM((3, 4 * cout, width), bf16),
            VMEM((2, 3 * cin, width), bf16),
            VMEM((2, 3 * cin, width), bf16),
            VMEM((3, 3 * cin, 3 * cout), bf16),
            VMEM((3, 3 * cin, 3 * cout), bf16),
            VMEM((2 * half, 128), f32),
            VMEM((half, 128), f32),
            VMEM((half, 128), f32),
            VMEM((2 * half, 128), f32),
            pltpu.SemaphoreType.DMA((10,)),
            pltpu.SemaphoreType.DMA((12,)),
            pltpu.SemaphoreType.DMA((8, count)),
        ],
        compiler_params=pltpu.CompilerParams(
            collective_id=0, has_side_effects=True, vmem_limit_bytes=40 * 2**20
        ),
    )(
        acts[:, 0].transpose(1, 0, 2),
        grad_out[:, 0].transpose(1, 0, 2),
        kernel.reshape(27, cin, cout),
    )
    return out.transpose(1, 0, 2)[:, None], wgrad.reshape(kernel.shape)


def solution(mesh):
    placed = (
        P(None, ("grp", "sp"), ("flt", "rep"), None),
        P(None, ("grp", "sp"), ("flt", "rep"), None),
        P(),
    )
    return jax.shard_map(
        per_device,
        mesh=mesh,
        in_specs=placed,
        out_specs=(P(None, ("grp", "sp"), ("flt", "rep"), None), P("grp", None, None, None, None)),
        check_vma=False,
    )
```

```python
import functools
import math

import jax
import jax.numpy as jnp
from jax import lax
from jax.experimental import pallas as pl
from jax.experimental.pallas import tpu as pltpu
from jax.sharding import PartitionSpec as P

MESH = pl.DeviceIdType.MESH
VMEM = pltpu.VMEM


class Group:
    def __init__(self, sp, flt):
        self.flt, self.count = flt, sp * flt
        self.core = lax.axis_index("rep")
        self.chip = lax.axis_index("sp") * flt + lax.axis_index("flt")

    def peer(self, chip):
        return {"sp": chip // self.flt, "flt": chip % self.flt}

    def partner(self):
        return {"rep": 1 - self.core}

    def after(self, step):
        return lax.rem(self.chip + 1 + step, self.count)

    def before(self, step):
        return lax.rem(self.chip + 2 * self.count - 1 - step, self.count)


def sum_over_group(group, piece, terms, held, arrived, total, sems):
    core, chip, count = group.core, group.chip, group.count
    half = count * piece

    def rows(at):
        return pl.ds(pl.multiple_of(at, 8), piece)

    def to_partner(j):
        return pltpu.make_async_remote_copy(
            terms.at[rows((1 - core) * half + j * piece)],
            held.at[rows(j * piece)],
            sems.at[0, j],
            sems.at[1, j],
            device_id=group.partner(),
            device_id_type=MESH,
        )

    def scatter(j, slot):
        return pltpu.make_async_remote_copy(
            held.at[rows(j * piece)],
            arrived.at[rows(slot * piece)],
            sems.at[2, j],
            sems.at[3, slot],
            device_id=group.peer(j),
            device_id_type=MESH,
        )

    def gather(j, slot):
        part = total.at[rows(core * half + slot * piece)]
        return pltpu.make_async_remote_copy(
            part,
            part,
            sems.at[4, j],
            sems.at[5, slot],
            device_id=group.peer(j),
            device_id_type=MESH,
        )

    def pass_on(j, owner):
        part = total.at[rows(owner * half + j * piece)]
        return pltpu.make_async_remote_copy(
            part,
            part,
            sems.at[6, j],
            sems.at[7, j],
            device_id=group.partner(),
            device_id_type=MESH,
        )

    def each(steps, body):
        def run(step, carry):
            body(step)
            return carry

        lax.fori_loop(0, steps, run, 0)

    def start():
        each(count, lambda k: to_partner(group.after(k)).start())

    def add_and_scatter(k):
        j = group.after(k)
        to_partner(j).wait_recv()
        own = rows(j * piece)
        held[own, :] = held[own, :] + terms[rows(core * half + j * piece), :]

        @pl.when(k < count - 1)
        def _():
            scatter(j, chip).start()

    def add_arrived(k):
        j = group.before(k)
        scatter(j, j).wait_recv()
        own = rows(chip * piece)
        held[own, :] = held[own, :] + arrived[rows(j * piece), :]

    def middle():
        each(count, add_and_scatter)

    def forward(k):
        j = group.before(k)
        gather(j, j).wait_recv()
        pass_on(j, core).start()

    def reduce():
        each(count - 1, add_arrived)
        total[rows(core * half + chip * piece), :] = held[rows(chip * piece), :]
        each(count - 1, lambda k: gather(group.after(k), chip).start())
        pass_on(chip, core).start()

    def finish():
        each(count - 1, forward)
        each(count, lambda k: pass_on(k, 1 - core).wait_recv())
        each(count, lambda k: to_partner(k).wait_send())
        each(count, lambda k: pass_on(k, core).wait_send())

        def sent(k):
            j = group.after(k)
            scatter(j, chip).wait_send()
            gather(j, chip).wait_send()

        each(count - 1, sent)

    return start, middle, reduce, finish


def halves(value):
    high = value.astype(jnp.bfloat16)
    return high, (value - high.astype(jnp.float32)).astype(jnp.bfloat16)


def moved(value, step):
    width = value.shape[-1]
    lane = lax.broadcasted_iota(jnp.int32, value.shape, 1)
    edge = 0 if step == 1 else width - 1
    return jnp.where(lane == edge, 0.0, pltpu.roll(value, step % width, 1))


def product(left, right, dims):
    (lh, ll), (rh, rl) = left, right

    def dot(x, y):
        return lax.dot_general(x, y, (dims, ((), ())), preferred_element_type=jnp.float32)

    return dot(lh, rh) + dot(lh, rl) + dot(ll, rh)


def backward_kernel(
    sp, flt, pieces, sizes, factor, acts, grad, weights, out, wgrad,
    pad, high, low, acts_high, acts_low, w_high, w_low,
    send, recv, *buffers,
):
    buffers = (buffers[:5], buffers[5:])
    group = Group(sp, flt)
    core, count = group.core, group.count
    z, x = lax.axis_index("sp"), lax.axis_index("flt")
    cin, width = acts.shape[1:]
    cout = grad.shape[1]
    halves_of = [count * piece for piece in pieces]
    z_exists = {0: z > 0, 2: z < sp - 1}
    cross_x = x + 2 * core - 1
    cross_exists = (cross_x >= 0) & (cross_x < flt)
    cross = {"flt": cross_x, "rep": 1 - core}

    barrier = pltpu.get_barrier_semaphore()
    pl.semaphore_signal(barrier, 1, device_id=group.partner(), device_id_type=MESH)

    def signal(k, carry):
        pl.semaphore_signal(
            barrier, 1, device_id=group.peer(group.after(k)), device_id_type=MESH
        )
        return carry

    lax.fori_loop(0, count - 1, signal, 0)

    @pl.when(cross_exists)
    def _():
        pl.semaphore_signal(barrier, 1, device_id=cross, device_id_type=MESH)
        pl.semaphore_wait(barrier, count + 1)

    @pl.when(jnp.logical_not(cross_exists))
    def _():
        pl.semaphore_wait(barrier, count)

    def copy(src, index, slot, device):
        return pltpu.make_async_remote_copy(
            src, pad.at[index], send.at[slot], recv.at[index],
            device_id=device, device_id_type=MESH,
        )

    def to_z(plane, row):
        return copy(grad.at[row], (2 - plane) * 4 + 1 + row, plane + row, {"sp": z + plane - 1})

    def edge(plane, row):
        return grad.at[row - 1] if plane == 1 else pad.at[plane * 4 + row]

    def to_cross(plane):
        return copy(edge(plane, 1 + core), plane * 4 + 3 * (1 - core), 4 + plane, cross)

    def to_partner(plane):
        return copy(edge(plane, 2 - core), plane * 4 + 3 * core, 7 + plane, group.partner())

    def await_row(plane, row):
        index = plane * 4 + row
        copy(grad.at[0], index, 0, group.partner()).wait_recv()

    for plane in (0, 2):

        @pl.when(z_exists[plane])
        def _():
            to_z(plane, core).start()

    @pl.when(cross_exists)
    def _():
        to_cross(1).start()

    to_partner(1).start()
    for plane in (0, 2):

        @pl.when(z_exists[plane])
        def _():
            to_z(plane, 1 - core).start()

    def keep(plane, row, value):
        at = pl.ds(pl.multiple_of(row * cout, cout), cout)
        high[plane, at, :], low[plane, at, :] = halves(value)

    for row in range(2):
        keep(1, 1 + row, grad[row])
        line = acts[row]
        for c, value in enumerate((moved(line, 1), line, moved(line, -1))):
            at = pl.ds(c * cin, cin)
            acts_high[row, at, :], acts_low[row, at, :] = halves(value)
    for a in range(3):
        for c in range(3):
            taps = jnp.concatenate([weights[9 * a + 3 * b + c] for b in (2, 1, 0)], axis=1)
            at = pl.ds(c * cin, cin)
            w_high[a, at, :], w_low[a, at, :] = halves(taps)

    def place(chunk, row):
        size = sizes[chunk]
        return row if row < size else row - size + halves_of[chunk]

    def put(chunk, row, value):
        terms, rows = buffers[chunk][0], value.shape[0]
        first = min(max(sizes[chunk] - row, 0), rows)
        if first:
            terms[pl.ds(row, first), :] = value[:first]
        if rows - first:
            terms[pl.ds(place(chunk, row + first), rows - first), :] = value[first:]

    for chunk in range(2):
        spare = halves_of[chunk] - sizes[chunk]
        for owner in range(2 if spare else 0):
            at = pl.ds(owner * halves_of[chunk] + sizes[chunk], spare)
            buffers[chunk][0][at, :] = jnp.zeros((spare, 128), jnp.float32)

    blocks = 3 * cout
    each_tap = 9 * cin * cout // 128
    base = ((1, each_tap), (0, 0), (1, 0))

    def weight_terms(a):
        plane = 2 - a
        result = jnp.zeros((3 * cin, blocks), jnp.float32)
        for row in range(2):
            at = pl.ds(row * cout, blocks)
            result = result + product(
                (acts_high[row], acts_low[row]),
                (high[plane, at, :], low[plane, at, :]),
                ((1,), (1,)),
            )
        chunk, at = base[a]
        put(chunk, at, result[:, :128])
        rest = result[:, 128:]
        middle = 3 * cin // 2
        put(chunk, at + 3 * cin, jnp.concatenate([rest[:middle], rest[middle:]], axis=1))

    def take(plane, row, exists):
        @pl.when(exists)
        def _():
            await_row(plane, row)
            keep(plane, row, pad[plane * 4 + row])

        @pl.when(jnp.logical_not(exists))
        def _():
            keep(plane, row, jnp.zeros((cout, width), jnp.float32))

    always = z >= 0
    for plane in (0, 2):

        @pl.when(z_exists[plane])
        def _():
            await_row(plane, 1 + core)

            @pl.when(cross_exists)
            def _():
                to_cross(plane).start()

    take(1, 3 * (1 - core), always)
    take(1, 3 * core, cross_exists)
    weight_terms(1)
    sums = [
        sum_over_group(group, pieces[i], *buffers[i]) for i in range(2)
    ]
    sums[0][0]()
    for plane in (0, 2):

        @pl.when(z_exists[plane])
        def _():
            await_row(plane, 2 - core)
            to_partner(plane).start()
            keep(plane, 1, pad[plane * 4 + 1])
            keep(plane, 2, pad[plane * 4 + 2])

        @pl.when(jnp.logical_not(z_exists[plane]))
        def _():
            for row in (1, 2):
                keep(plane, row, jnp.zeros((cout, width), jnp.float32))

    sums[0][1]()
    for plane in (0, 2):
        take(plane, 3 * (1 - core), z_exists[plane])
        take(plane, 3 * core, z_exists[plane] & cross_exists)
        weight_terms(2 - plane)

    sums[1][0]()
    sums[0][2]()
    sums[1][1]()
    for row in range(2):
        at = pl.ds(row * cout, blocks)
        result = jnp.zeros((3 * cin, width), jnp.float32)
        for a in range(3):
            result = result + product(
                (w_high[a], w_low[a]), (high[2 - a, at, :], low[2 - a, at, :]), ((1,), (0,))
            )
        out[row] = (
            moved(result[:cin], -1) + result[cin : 2 * cin] + moved(result[2 * cin :], 1)
        )
    sums[1][2]()
    for plane in (0, 2):

        @pl.when(z_exists[plane])
        def _():
            to_z(plane, core).wait_send()
            to_z(plane, 1 - core).wait_send()
            to_partner(plane).wait_send()

        @pl.when(z_exists[plane] & cross_exists)
        def _():
            to_cross(plane).wait_send()

    to_partner(1).wait_send()

    @pl.when(cross_exists)
    def _():
        to_cross(1).wait_send()

    sums[0][3]()
    sums[1][3]()
    step = 16
    for a in range(3):
        for c in range(3):
            for i in range(0, cin, step):
                line = c * cin + i
                chunk, first = base[a]
                total = buffers[chunk][3]
                both = total[pl.ds(place(chunk, first + line), step), :] * factor
                wrapped, lane = line % (3 * cin // 2), line // (3 * cin // 2) * cout
                last = total[pl.ds(place(chunk, first + 3 * cin + wrapped), step), :] * factor
                at = pl.ds(i, step)
                wgrad[9 * a + 6 + c, at, :] = both[:, :cout]
                wgrad[9 * a + 3 + c, at, :] = both[:, cout:]
                wgrad[9 * a + c, at, :] = last[:, lane : lane + cout]


def per_device(acts, grad_out, kernel):
    cin, planes, rows, width = acts.shape
    cout = grad_out.shape[0]
    sp, flt = lax.axis_size("sp"), lax.axis_size("flt")
    count = sp * flt
    voxels = planes * sp * rows * flt * lax.axis_size("rep") * width
    factor = 1.0 / math.sqrt(voxels)
    sizes = (kernel.size // 256 // 3, kernel.size // 256 * 2 // 3)
    pieces = tuple(-(-size // (8 * count)) * 8 for size in sizes)
    f32, bf16 = jnp.float32, jnp.bfloat16
    vmem = pl.BlockSpec(memory_space=VMEM)
    out, wgrad = pl.pallas_call(
        functools.partial(backward_kernel, sp, flt, pieces, sizes, factor),
        out_shape=(
            jax.ShapeDtypeStruct((rows, cin, width), f32),
            jax.ShapeDtypeStruct((27, cin, cout), f32),
        ),
        in_specs=[vmem] * 3,
        out_specs=(vmem, vmem),
        scratch_shapes=[
            VMEM((12, cout, width), f32),
            VMEM((3, 4 * cout, width), bf16),
            VMEM((3, 4 * cout, width), bf16),
            VMEM((2, 3 * cin, width), bf16),
            VMEM((2, 3 * cin, width), bf16),
            VMEM((3, 3 * cin, 3 * cout), bf16),
            VMEM((3, 3 * cin, 3 * cout), bf16),
            pltpu.SemaphoreType.DMA((10,)),
            pltpu.SemaphoreType.DMA((12,)),
        ] + [
            kind
            for piece in pieces
            for kind in (
                VMEM((2 * count * piece, 128), f32),
                VMEM((count * piece, 128), f32),
                VMEM((count * piece, 128), f32),
                VMEM((2 * count * piece, 128), f32),
                pltpu.SemaphoreType.DMA((8, count)),
            )
        ],
        compiler_params=pltpu.CompilerParams(
            collective_id=0, has_side_effects=True, vmem_limit_bytes=40 * 2**20
        ),
    )(
        acts[:, 0].transpose(1, 0, 2),
        grad_out[:, 0].transpose(1, 0, 2),
        kernel.reshape(27, cin, cout),
    )
    return out.transpose(1, 0, 2)[:, None], wgrad.reshape(kernel.shape)


def solution(mesh):
    placed = (
        P(None, ("grp", "sp"), ("flt", "rep"), None),
        P(None, ("grp", "sp"), ("flt", "rep"), None),
        P(),
    )
    return jax.shard_map(
        per_device,
        mesh=mesh,
        in_specs=placed,
        out_specs=(P(None, ("grp", "sp"), ("flt", "rep"), None), P("grp", None, None, None, None)),
        check_vma=False,
    )
```

```python
import functools
import math

import jax
import jax.numpy as jnp
from jax import lax
from jax.experimental import pallas as pl
from jax.experimental.pallas import tpu as pltpu
from jax.sharding import PartitionSpec as P

MESH = pl.DeviceIdType.MESH
VMEM = pltpu.VMEM


class Group:
    def __init__(self, sp, flt):
        self.flt, self.count = flt, sp * flt
        self.core = lax.axis_index("rep")
        self.chip = lax.axis_index("sp") * flt + lax.axis_index("flt")

    def peer(self, chip):
        return {"sp": chip // self.flt, "flt": chip % self.flt}

    def partner(self):
        return {"rep": 1 - self.core}

    def after(self, step):
        return lax.rem(self.chip + 1 + step, self.count)

    def before(self, step):
        return lax.rem(self.chip + 2 * self.count - 1 - step, self.count)


def sum_over_group(group, piece, share, terms, held, arrived, total, sems):
    core, chip, count = group.core, group.chip, group.count
    half = count * piece

    def rows(at):
        return pl.ds(pl.multiple_of(at, 8), piece)

    def to_partner(j):
        return pltpu.make_async_remote_copy(
            terms.at[pl.ds(pl.multiple_of((1 - core) * half + j * share, 8), share)],
            held.at[pl.ds(j * share, share)],
            sems.at[0, j],
            sems.at[1, j],
            device_id=group.partner(),
            device_id_type=MESH,
        )

    def scatter(j, slot):
        return pltpu.make_async_remote_copy(
            held.at[rows(j * piece)],
            arrived.at[rows(slot * piece)],
            sems.at[2, j],
            sems.at[3, slot],
            device_id=group.peer(j),
            device_id_type=MESH,
        )

    def gather(j, slot):
        part = total.at[rows(core * half + slot * piece)]
        return pltpu.make_async_remote_copy(
            part,
            part,
            sems.at[4, j],
            sems.at[5, slot],
            device_id=group.peer(j),
            device_id_type=MESH,
        )

    def pass_on(j, owner):
        part = total.at[rows(owner * half + j * piece)]
        return pltpu.make_async_remote_copy(
            part,
            part,
            sems.at[6, j],
            sems.at[7, j],
            device_id=group.partner(),
            device_id_type=MESH,
        )

    def each(steps, body):
        def run(step, carry):
            body(step)
            return carry

        lax.fori_loop(0, steps, run, 0)

    def start(a):
        to_partner(a).start()

    def add_and_scatter(k):
        j = group.after(k)
        own = rows(j * piece)
        held[own, :] = held[own, :] + terms[rows(core * half + j * piece), :]

        @pl.when(k < count - 1)
        def _():
            scatter(j, chip).start()

    def add_arrived(k):
        j = group.before(k)
        scatter(j, j).wait_recv()
        own = rows(chip * piece)
        held[own, :] = held[own, :] + arrived[rows(j * piece), :]

    def middle():
        for a in range(3):
            to_partner(a).wait_recv()
        each(count, add_and_scatter)

    def forward(k):
        j = group.before(k)
        gather(j, j).wait_recv()
        pass_on(j, core).start()

    def finish():
        each(count - 1, add_arrived)
        total[rows(core * half + chip * piece), :] = held[rows(chip * piece), :]
        each(count - 1, lambda k: gather(group.after(k), chip).start())
        pass_on(chip, core).start()
        each(count - 1, forward)
        each(count, lambda k: pass_on(k, 1 - core).wait_recv())
        for a in range(3):
            to_partner(a).wait_send()
        each(count, lambda k: pass_on(k, core).wait_send())

        def sent(k):
            j = group.after(k)
            scatter(j, chip).wait_send()
            gather(j, chip).wait_send()

        each(count - 1, sent)

    return start, middle, finish


def halves(value):
    high = value.astype(jnp.bfloat16)
    return high, (value - high.astype(jnp.float32)).astype(jnp.bfloat16)


def moved(value, step):
    width = value.shape[-1]
    lane = lax.broadcasted_iota(jnp.int32, value.shape, 1)
    edge = 0 if step == 1 else width - 1
    return jnp.where(lane == edge, 0.0, pltpu.roll(value, step % width, 1))


def product(left, right, dims):
    (lh, ll), (rh, rl) = left, right

    def dot(x, y):
        return lax.dot_general(x, y, (dims, ((), ())), preferred_element_type=jnp.float32)

    return dot(lh, rh) + dot(lh, rl) + dot(ll, rh)


def backward_kernel(
    sp, flt, piece, size, factor, acts, grad, weights, out, wgrad,
    pad, high, low, acts_high, acts_low, w_high, w_low,
    terms, held, arrived, total, send, recv, sems,
):
    group = Group(sp, flt)
    core, count = group.core, group.count
    z, x = lax.axis_index("sp"), lax.axis_index("flt")
    cin, width = acts.shape[1:]
    cout = grad.shape[1]
    half = count * piece
    z_exists = {0: z > 0, 2: z < sp - 1}
    cross_x = x + 2 * core - 1
    cross_exists = (cross_x >= 0) & (cross_x < flt)
    cross = {"flt": cross_x, "rep": 1 - core}

    barrier = pltpu.get_barrier_semaphore()
    pl.semaphore_signal(barrier, 1, device_id=group.partner(), device_id_type=MESH)

    def signal(k, carry):
        pl.semaphore_signal(
            barrier, 1, device_id=group.peer(group.after(k)), device_id_type=MESH
        )
        return carry

    lax.fori_loop(0, count - 1, signal, 0)

    @pl.when(cross_exists)
    def _():
        pl.semaphore_signal(barrier, 1, device_id=cross, device_id_type=MESH)
        pl.semaphore_wait(barrier, count + 1)

    @pl.when(jnp.logical_not(cross_exists))
    def _():
        pl.semaphore_wait(barrier, count)

    def copy(src, index, slot, device):
        return pltpu.make_async_remote_copy(
            src, pad.at[index], send.at[slot], recv.at[index],
            device_id=device, device_id_type=MESH,
        )

    def to_z(plane, row):
        return copy(grad.at[row], (2 - plane) * 4 + 1 + row, plane + row, {"sp": z + plane - 1})

    def edge(plane, row):
        return grad.at[row - 1] if plane == 1 else pad.at[plane * 4 + row]

    def to_cross(plane):
        return copy(edge(plane, 1 + core), plane * 4 + 3 * (1 - core), 4 + plane, cross)

    def to_partner(plane):
        return copy(edge(plane, 2 - core), plane * 4 + 3 * core, 7 + plane, group.partner())

    def await_row(plane, row):
        index = plane * 4 + row
        copy(grad.at[0], index, 0, group.partner()).wait_recv()

    for plane in (0, 2):

        @pl.when(z_exists[plane])
        def _():
            to_z(plane, core).start()

    @pl.when(cross_exists)
    def _():
        to_cross(1).start()

    to_partner(1).start()
    for plane in (0, 2):

        @pl.when(z_exists[plane])
        def _():
            to_z(plane, 1 - core).start()

    def keep(plane, row, value):
        at = pl.ds(pl.multiple_of(row * cout, cout), cout)
        high[plane, at, :], low[plane, at, :] = halves(value)

    for row in range(2):
        keep(1, 1 + row, grad[row])
        line = acts[row]
        for c, value in enumerate((moved(line, 1), line, moved(line, -1))):
            at = pl.ds(c * cin, cin)
            acts_high[row, at, :], acts_low[row, at, :] = halves(value)
    for a in range(3):
        for c in range(3):
            taps = jnp.concatenate([weights[9 * a + 3 * b + c] for b in (2, 1, 0)], axis=1)
            at = pl.ds(c * cin, cin)
            w_high[a, at, :], w_low[a, at, :] = halves(taps)

    share = size // 3

    def place(a, row):
        return row // share * half + a * share + row % share

    def put(a, row, value):
        rows = value.shape[0]
        first = min(max(share - row, 0), rows)
        if first:
            terms[pl.ds(place(a, row), first), :] = value[:first]
        if rows - first:
            terms[pl.ds(place(a, row + first), rows - first), :] = value[first:]

    if half > size:
        spare = jnp.zeros((half - size, 128), jnp.float32)
        held[pl.ds(size, half - size), :] = spare
        for owner in range(2):
            terms[pl.ds(owner * half + size, half - size), :] = spare

    start, middle, finish = sum_over_group(
        group, piece, share, terms, held, arrived, total, sems
    )
    blocks = 3 * cout

    def weight_terms(a):
        plane = 2 - a
        result = jnp.zeros((3 * cin, blocks), jnp.float32)
        for row in range(2):
            at = pl.ds(row * cout, blocks)
            result = result + product(
                (acts_high[row], acts_low[row]),
                (high[plane, at, :], low[plane, at, :]),
                ((1,), (1,)),
            )
        put(a, 0, result[:, :128])
        rest = result[:, 128:]
        split = 3 * cin // 2
        put(a, 3 * cin, jnp.concatenate([rest[:split], rest[split:]], axis=1))
        start(a)

    def take(plane, row, exists):
        @pl.when(exists)
        def _():
            await_row(plane, row)
            keep(plane, row, pad[plane * 4 + row])

        @pl.when(jnp.logical_not(exists))
        def _():
            keep(plane, row, jnp.zeros((cout, width), jnp.float32))

    always = z >= 0
    for plane in (0, 2):

        @pl.when(z_exists[plane])
        def _():
            await_row(plane, 1 + core)

            @pl.when(cross_exists)
            def _():
                to_cross(plane).start()

    take(1, 3 * (1 - core), always)
    take(1, 3 * core, cross_exists)
    weight_terms(1)
    for plane in (0, 2):

        @pl.when(z_exists[plane])
        def _():
            await_row(plane, 2 - core)
            to_partner(plane).start()
            keep(plane, 1, pad[plane * 4 + 1])
            keep(plane, 2, pad[plane * 4 + 2])

        @pl.when(jnp.logical_not(z_exists[plane]))
        def _():
            for row in (1, 2):
                keep(plane, row, jnp.zeros((cout, width), jnp.float32))

    for plane in (0, 2):
        take(plane, 3 * (1 - core), z_exists[plane])
        take(plane, 3 * core, z_exists[plane] & cross_exists)
        weight_terms(2 - plane)

    middle()
    for row in range(2):
        at = pl.ds(row * cout, blocks)
        result = jnp.zeros((3 * cin, width), jnp.float32)
        for a in range(3):
            result = result + product(
                (w_high[a], w_low[a]), (high[2 - a, at, :], low[2 - a, at, :]), ((1,), (0,))
            )
        out[row] = (
            moved(result[:cin], -1) + result[cin : 2 * cin] + moved(result[2 * cin :], 1)
        )
    for plane in (0, 2):

        @pl.when(z_exists[plane])
        def _():
            to_z(plane, core).wait_send()
            to_z(plane, 1 - core).wait_send()
            to_partner(plane).wait_send()

        @pl.when(z_exists[plane] & cross_exists)
        def _():
            to_cross(plane).wait_send()

    to_partner(1).wait_send()

    @pl.when(cross_exists)
    def _():
        to_cross(1).wait_send()

    finish()
    step = 16
    for a in range(3):
        for c in range(3):
            for i in range(0, cin, step):
                line = c * cin + i
                both = total[pl.ds(place(a, line), step), :] * factor
                wrapped, lane = line % (3 * cin // 2), line // (3 * cin // 2) * cout
                last = total[pl.ds(place(a, 3 * cin + wrapped), step), :] * factor
                at = pl.ds(i, step)
                wgrad[9 * a + 6 + c, at, :] = both[:, :cout]
                wgrad[9 * a + 3 + c, at, :] = both[:, cout:]
                wgrad[9 * a + c, at, :] = last[:, lane : lane + cout]


def per_device(acts, grad_out, kernel):
    cin, planes, rows, width = acts.shape
    cout = grad_out.shape[0]
    sp, flt = lax.axis_size("sp"), lax.axis_size("flt")
    count = sp * flt
    voxels = planes * sp * rows * flt * lax.axis_size("rep") * width
    factor = 1.0 / math.sqrt(voxels)
    size = kernel.size // 256
    piece = -(-size // (8 * count)) * 8
    half = count * piece
    f32, bf16 = jnp.float32, jnp.bfloat16
    vmem = pl.BlockSpec(memory_space=VMEM)
    out, wgrad = pl.pallas_call(
        functools.partial(backward_kernel, sp, flt, piece, size, factor),
        out_shape=(
            jax.ShapeDtypeStruct((rows, cin, width), f32),
            jax.ShapeDtypeStruct((27, cin, cout), f32),
        ),
        in_specs=[vmem] * 3,
        out_specs=(vmem, vmem),
        scratch_shapes=[
            VMEM((12, cout, width), f32),
            VMEM((3, 4 * cout, width), bf16),
            VMEM((3, 4 * cout, width), bf16),
            VMEM((2, 3 * cin, width), bf16),
            VMEM((2, 3 * cin, width), bf16),
            VMEM((3, 3 * cin, 3 * cout), bf16),
            VMEM((3, 3 * cin, 3 * cout), bf16),
            VMEM((2 * half, 128), f32),
            VMEM((half, 128), f32),
            VMEM((half, 128), f32),
            VMEM((2 * half, 128), f32),
            pltpu.SemaphoreType.DMA((10,)),
            pltpu.SemaphoreType.DMA((12,)),
            pltpu.SemaphoreType.DMA((8, max(count, 3))),
        ],
        compiler_params=pltpu.CompilerParams(
            collective_id=0, has_side_effects=True, vmem_limit_bytes=40 * 2**20
        ),
    )(
        acts[:, 0].transpose(1, 0, 2),
        grad_out[:, 0].transpose(1, 0, 2),
        kernel.reshape(27, cin, cout),
    )
    return out.transpose(1, 0, 2)[:, None], wgrad.reshape(kernel.shape)


def solution(mesh):
    placed = (
        P(None, ("grp", "sp"), ("flt", "rep"), None),
        P(None, ("grp", "sp"), ("flt", "rep"), None),
        P(),
    )
    return jax.shard_map(
        per_device,
        mesh=mesh,
        in_specs=placed,
        out_specs=(P(None, ("grp", "sp"), ("flt", "rep"), None), P("grp", None, None, None, None)),
        check_vma=False,
    )
```

```python
import functools
import math

import jax
import jax.numpy as jnp
from jax import lax
from jax.experimental import pallas as pl
from jax.experimental.pallas import tpu as pltpu
from jax.sharding import PartitionSpec as P

MESH = pl.DeviceIdType.MESH
VMEM = pltpu.VMEM


class Group:
    def __init__(self, sp, flt):
        self.sp, self.count = sp, sp * flt
        self.core = lax.axis_index("rep")
        self.chip = lax.axis_index("flt") * sp + lax.axis_index("sp")

    def peer(self, chip):
        return {"sp": chip % self.sp, "flt": chip // self.sp}

    def partner(self):
        return {"rep": 1 - self.core}

    def after(self, step):
        return lax.rem(self.chip + 1 + step, self.count)

    def before(self, step):
        return lax.rem(self.chip + 2 * self.count - 1 - step, self.count)


def sum_over_group(group, piece, terms, held, arrived, total, sems):
    core, chip, count = group.core, group.chip, group.count
    half = count * piece

    def rows(at):
        return pl.ds(pl.multiple_of(at, 8), piece)

    def to_partner(j):
        return pltpu.make_async_remote_copy(
            terms.at[rows((1 - core) * half + j * piece)],
            held.at[rows(j * piece)],
            sems.at[0, j],
            sems.at[1, j],
            device_id=group.partner(),
            device_id_type=MESH,
        )

    def scatter(j, slot):
        return pltpu.make_async_remote_copy(
            held.at[rows(j * piece)],
            arrived.at[rows(slot * piece)],
            sems.at[2, j],
            sems.at[3, slot],
            device_id=group.peer(j),
            device_id_type=MESH,
        )

    def gather(j, slot):
        part = total.at[rows(core * half + slot * piece)]
        return pltpu.make_async_remote_copy(
            part,
            part,
            sems.at[4, j],
            sems.at[5, slot],
            device_id=group.peer(j),
            device_id_type=MESH,
        )

    def pass_on(j, owner):
        part = total.at[rows(owner * half + j * piece)]
        return pltpu.make_async_remote_copy(
            part,
            part,
            sems.at[6, j],
            sems.at[7, j],
            device_id=group.partner(),
            device_id_type=MESH,
        )

    def each(steps, body):
        def run(step, carry):
            body(step)
            return carry

        lax.fori_loop(0, steps, run, 0)

    def start():
        each(count, lambda k: to_partner(group.after(k)).start())

    def add_and_scatter(k):
        j = group.after(k)
        to_partner(j).wait_recv()
        own = rows(j * piece)
        held[own, :] = held[own, :] + terms[rows(core * half + j * piece), :]

        @pl.when(k < count - 1)
        def _():
            scatter(j, chip).start()

    def add_arrived(k):
        j = group.before(k)
        scatter(j, j).wait_recv()
        own = rows(chip * piece)
        held[own, :] = held[own, :] + arrived[rows(j * piece), :]

    def middle():
        each(count, add_and_scatter)

    def forward(k):
        j = group.before(k)
        gather(j, j).wait_recv()
        pass_on(j, core).start()

    def finish():
        each(count - 1, add_arrived)
        total[rows(core * half + chip * piece), :] = held[rows(chip * piece), :]
        pass_on(chip, core).start()
        each(count - 1, lambda k: gather(group.after(k), chip).start())
        each(count - 1, forward)
        each(count, lambda k: pass_on(k, 1 - core).wait_recv())
        each(count, lambda k: to_partner(k).wait_send())
        each(count, lambda k: pass_on(k, core).wait_send())

        def sent(k):
            j = group.after(k)
            scatter(j, chip).wait_send()
            gather(j, chip).wait_send()

        each(count - 1, sent)

    return start, middle, finish


def halves(value):
    high = value.astype(jnp.bfloat16)
    return high, (value - high.astype(jnp.float32)).astype(jnp.bfloat16)


def moved(value, step):
    width = value.shape[-1]
    lane = lax.broadcasted_iota(jnp.int32, value.shape, 1)
    edge = 0 if step == 1 else width - 1
    return jnp.where(lane == edge, 0.0, pltpu.roll(value, step % width, 1))


def product(left, right, dims):
    (lh, ll), (rh, rl) = left, right

    def dot(x, y):
        return lax.dot_general(x, y, (dims, ((), ())), preferred_element_type=jnp.float32)

    return dot(lh, rh) + dot(lh, rl) + dot(ll, rh)


def backward_kernel(
    sp, flt, piece, size, factor, acts, grad, weights, out, wgrad,
    pad, high, low, acts_high, acts_low, w_high, w_low,
    terms, held, arrived, total, send, recv, sems,
):
    group = Group(sp, flt)
    core, count = group.core, group.count
    z, x = lax.axis_index("sp"), lax.axis_index("flt")
    cin, width = acts.shape[1:]
    cout = grad.shape[1]
    half = count * piece
    z_exists = {0: z > 0, 2: z < sp - 1}
    cross_x = x + 2 * core - 1
    cross_exists = (cross_x >= 0) & (cross_x < flt)
    cross = {"flt": cross_x, "rep": 1 - core}

    barrier = pltpu.get_barrier_semaphore()
    pl.semaphore_signal(barrier, 1, device_id=group.partner(), device_id_type=MESH)

    def signal(k, carry):
        pl.semaphore_signal(
            barrier, 1, device_id=group.peer(group.after(k)), device_id_type=MESH
        )
        return carry

    lax.fori_loop(0, count - 1, signal, 0)

    @pl.when(cross_exists)
    def _():
        pl.semaphore_signal(barrier, 1, device_id=cross, device_id_type=MESH)
        pl.semaphore_wait(barrier, count + 1)

    @pl.when(jnp.logical_not(cross_exists))
    def _():
        pl.semaphore_wait(barrier, count)

    def copy(src, index, slot, device):
        return pltpu.make_async_remote_copy(
            src, pad.at[index], send.at[slot], recv.at[index],
            device_id=device, device_id_type=MESH,
        )

    def to_z(plane, row):
        return copy(grad.at[row], (2 - plane) * 4 + 1 + row, plane + row, {"sp": z + plane - 1})

    def edge(plane, row):
        return grad.at[row - 1] if plane == 1 else pad.at[plane * 4 + row]

    def to_cross(plane):
        return copy(edge(plane, 1 + core), plane * 4 + 3 * (1 - core), 4 + plane, cross)

    def to_partner(plane):
        return copy(edge(plane, 2 - core), plane * 4 + 3 * core, 7 + plane, group.partner())

    def await_row(plane, row):
        index = plane * 4 + row
        copy(grad.at[0], index, 0, group.partner()).wait_recv()

    for plane in (0, 2):

        @pl.when(z_exists[plane])
        def _():
            to_z(plane, core).start()

    @pl.when(cross_exists)
    def _():
        to_cross(1).start()

    to_partner(1).start()
    for plane in (0, 2):

        @pl.when(z_exists[plane])
        def _():
            to_z(plane, 1 - core).start()

    def keep(plane, row, value):
        at = pl.ds(pl.multiple_of(row * cout, cout), cout)
        high[plane, at, :], low[plane, at, :] = halves(value)

    for row in range(2):
        keep(1, 1 + row, grad[row])
        line = acts[row]
        for c, value in enumerate((moved(line, 1), line, moved(line, -1))):
            at = pl.ds(c * cin, cin)
            acts_high[row, at, :], acts_low[row, at, :] = halves(value)
    for a in range(3):
        for c in range(3):
            taps = jnp.concatenate([weights[9 * a + 3 * b + c] for b in (2, 1, 0)], axis=1)
            at = pl.ds(c * cin, cin)
            w_high[a, at, :], w_low[a, at, :] = halves(taps)

    def place(row):
        return row if row < size else row - size + half

    def put(row, value):
        rows = value.shape[0]
        first = min(max(size - row, 0), rows)
        if first:
            terms[pl.ds(row, first), :] = value[:first]
        if rows - first:
            terms[pl.ds(place(row + first), rows - first), :] = value[first:]

    if half > size:
        for owner in range(2):
            terms[pl.ds(owner * half + size, half - size), :] = jnp.zeros(
                (half - size, 128), jnp.float32
            )

    blocks = 3 * cout
    each_tap = 9 * cin * cout // 128

    def weight_terms(a):
        plane = 2 - a
        result = jnp.zeros((3 * cin, blocks), jnp.float32)
        for row in range(2):
            at = pl.ds(row * cout, blocks)
            result = result + product(
                (acts_high[row], acts_low[row]),
                (high[plane, at, :], low[plane, at, :]),
                ((1,), (1,)),
            )
        put(a * each_tap, result[:, :128])
        rest = result[:, 128:]
        middle = 3 * cin // 2
        put(a * each_tap + 3 * cin, jnp.concatenate([rest[:middle], rest[middle:]], axis=1))

    def take(plane, row, exists):
        @pl.when(exists)
        def _():
            await_row(plane, row)
            keep(plane, row, pad[plane * 4 + row])

        @pl.when(jnp.logical_not(exists))
        def _():
            keep(plane, row, jnp.zeros((cout, width), jnp.float32))

    always = z >= 0
    for plane in (0, 2):

        @pl.when(z_exists[plane])
        def _():
            await_row(plane, 1 + core)

            @pl.when(cross_exists)
            def _():
                to_cross(plane).start()

    take(1, 3 * (1 - core), always)
    take(1, 3 * core, cross_exists)
    weight_terms(1)
    for plane in (0, 2):

        @pl.when(z_exists[plane])
        def _():
            await_row(plane, 2 - core)
            to_partner(plane).start()
            keep(plane, 1, pad[plane * 4 + 1])
            keep(plane, 2, pad[plane * 4 + 2])

        @pl.when(jnp.logical_not(z_exists[plane]))
        def _():
            for row in (1, 2):
                keep(plane, row, jnp.zeros((cout, width), jnp.float32))

    for plane in (0, 2):
        take(plane, 3 * (1 - core), z_exists[plane])
        take(plane, 3 * core, z_exists[plane] & cross_exists)
        weight_terms(2 - plane)

    start, middle, finish = sum_over_group(group, piece, terms, held, arrived, total, sems)
    start()
    middle()
    for row in range(2):
        at = pl.ds(row * cout, blocks)
        result = jnp.zeros((3 * cin, width), jnp.float32)
        for a in range(3):
            result = result + product(
                (w_high[a], w_low[a]), (high[2 - a, at, :], low[2 - a, at, :]), ((1,), (0,))
            )
        out[row] = (
            moved(result[:cin], -1) + result[cin : 2 * cin] + moved(result[2 * cin :], 1)
        )
    for plane in (0, 2):

        @pl.when(z_exists[plane])
        def _():
            to_z(plane, core).wait_send()
            to_z(plane, 1 - core).wait_send()
            to_partner(plane).wait_send()

        @pl.when(z_exists[plane] & cross_exists)
        def _():
            to_cross(plane).wait_send()

    to_partner(1).wait_send()

    @pl.when(cross_exists)
    def _():
        to_cross(1).wait_send()

    finish()
    step = 16
    for a in range(3):
        for c in range(3):
            for i in range(0, cin, step):
                line = c * cin + i
                both = total[pl.ds(place(a * each_tap + line), step), :] * factor
                wrapped, lane = line % (3 * cin // 2), line // (3 * cin // 2) * cout
                last = total[pl.ds(place(a * each_tap + 3 * cin + wrapped), step), :] * factor
                at = pl.ds(i, step)
                wgrad[9 * a + 6 + c, at, :] = both[:, :cout]
                wgrad[9 * a + 3 + c, at, :] = both[:, cout:]
                wgrad[9 * a + c, at, :] = last[:, lane : lane + cout]


def per_device(acts, grad_out, kernel):
    cin, planes, rows, width = acts.shape
    cout = grad_out.shape[0]
    sp, flt = lax.axis_size("sp"), lax.axis_size("flt")
    count = sp * flt
    voxels = planes * sp * rows * flt * lax.axis_size("rep") * width
    factor = 1.0 / math.sqrt(voxels)
    size = kernel.size // 256
    piece = -(-size // (8 * count)) * 8
    half = count * piece
    f32, bf16 = jnp.float32, jnp.bfloat16
    vmem = pl.BlockSpec(memory_space=VMEM)
    out, wgrad = pl.pallas_call(
        functools.partial(backward_kernel, sp, flt, piece, size, factor),
        out_shape=(
            jax.ShapeDtypeStruct((rows, cin, width), f32),
            jax.ShapeDtypeStruct((27, cin, cout), f32),
        ),
        in_specs=[vmem] * 3,
        out_specs=(vmem, vmem),
        scratch_shapes=[
            VMEM((12, cout, width), f32),
            VMEM((3, 4 * cout, width), bf16),
            VMEM((3, 4 * cout, width), bf16),
            VMEM((2, 3 * cin, width), bf16),
            VMEM((2, 3 * cin, width), bf16),
            VMEM((3, 3 * cin, 3 * cout), bf16),
            VMEM((3, 3 * cin, 3 * cout), bf16),
            VMEM((2 * half, 128), f32),
            VMEM((half, 128), f32),
            VMEM((half, 128), f32),
            VMEM((2 * half, 128), f32),
            pltpu.SemaphoreType.DMA((10,)),
            pltpu.SemaphoreType.DMA((12,)),
            pltpu.SemaphoreType.DMA((8, count)),
        ],
        compiler_params=pltpu.CompilerParams(
            collective_id=0, has_side_effects=True, vmem_limit_bytes=40 * 2**20
        ),
    )(
        acts[:, 0].transpose(1, 0, 2),
        grad_out[:, 0].transpose(1, 0, 2),
        kernel.reshape(27, cin, cout),
    )
    return out.transpose(1, 0, 2)[:, None], wgrad.reshape(kernel.shape)


def solution(mesh):
    placed = (
        P(None, ("grp", "sp"), ("flt", "rep"), None),
        P(None, ("grp", "sp"), ("flt", "rep"), None),
        P(),
    )
    return jax.shard_map(
        per_device,
        mesh=mesh,
        in_specs=placed,
        out_specs=(P(None, ("grp", "sp"), ("flt", "rep"), None), P("grp", None, None, None, None)),
        check_vma=False,
    )
```
